128 devices in a mesh: lat: 8 (over y_lo, x), lon: 16 (over y_hi, z, core).
Axes of the slice: x: 4, y: 4 (y_hi: 2, y_lo: 2; y = y_hi * 2 + y_lo), z: 4, core: 2. Of those that a mesh axis runs over, the one named last changes fastest.
Arguments:
- inputs: float32 [1, 128, 256, 384], P(None, 'lat', 'lon'), may hold values from -6 to 6
- saved: float32 [1, 128, 256, 384], P(None, 'lat', 'lon'), may hold values from -6 to 6
- grad_out: float32 [1, 128, 256, 384], P(None, 'lat', 'lon'), may hold values from -6 to 6
- w_up: float32 [384, 768], replicated, may hold values from -0.3125 to 0.3125
- w_down: float32 [768, 384], replicated, may hold values from -0.21875 to 0.21875
- w_filter: float32 [128, 384, 384], P('lon'), may hold values from -0.3125 to 0.3125
Outputs:
- grad_input: float32 [1, 128, 256, 384], P(None, 'lat', 'lon')
- grad_up: float32 [384, 768], P(None, ('lat', 'lon'))
- grad_down: float32 [768, 384], P(('lat', 'lon'))
- grad_filter: float32 [128, 384, 384], P('lon', 'lat')
The draws below stay inside these ranges and needn't reach their ends.
All inputs are finite; a program needn't handle non-finite values.
Results may differ from the reference program's by a relative error of at most 0.0003.
Values sent between devices are 32-bit elements; how exact they have to be, the bound alone decides.
A program may use at most 128 MiB of HBM per device.

```python
import math
import jax
import jax.numpy as jnp
from jax import lax

NLAT = 128
NLON = 256
MODES = 128
WIDTH = 384
HIDDEN_SIZE = 768
SAMPLES = 1


def block_levels(stream_key, dims, split, low, high):
    level = 1.0
    for dim, shards_of in split:
        steps = jax.random.uniform(jax.random.fold_in(jax.random.fold_in(stream_key, 6), dim), (shards_of,), jnp.float32, low / len(split), high / len(split))
        level = level * jnp.repeat(jnp.exp(steps), dims[dim] // shards_of).reshape((-1,) + (1,) * (len(dims) - 1 - dim))
    return level


def normal_values(stream_key, shape, scale, limit, pieces=(), kind=jnp.bfloat16):
    drawn = jax.random.normal(stream_key, shape, jnp.float32) * scale
    if len(pieces) > 0:
        drawn = block_levels(stream_key, shape, pieces, -0.22, 0.18) * drawn
    return jnp.clip(drawn, min=-limit, max=limit).astype(kind)


def setup_inputs(seed: int = 0) -> dict:
    splits = jax.random.split(jax.random.key(seed), 7)
    return {
        "inputs": normal_values(splits[0], (SAMPLES, NLAT, NLON, WIDTH), 1.0, 6.0, ((1, 8), (2, 16)), jnp.float32),
        "saved": normal_values(splits[1], (SAMPLES, NLAT, NLON, WIDTH), 1.0, 6.0, ((1, 8), (2, 16)), jnp.float32),
        "grad_out": normal_values(splits[2], (SAMPLES, NLAT, NLON, WIDTH), 1.0, 6.0, ((1, 8), (2, 16)), jnp.float32),
        "w_up": normal_values(splits[3], (WIDTH, HIDDEN_SIZE), WIDTH ** -0.5, 0.3125, (), jnp.float32),
        "w_down": normal_values(splits[4], (HIDDEN_SIZE, WIDTH), HIDDEN_SIZE ** -0.5, 0.21875, (), jnp.float32),
        "w_filter": normal_values(splits[5], (MODES, WIDTH, WIDTH), WIDTH ** -0.5, 0.3125, ((0, 16),), jnp.float32),
    }


HIGHEST = lax.Precision.HIGHEST

def legendre_table(first, count):
    row_ids = jnp.arange(NLAT, dtype=jnp.int32).astype(jnp.float32)
    colatitude = math.pi * (row_ids + 0.5) / NLAT
    cosines = jnp.cos(colatitude)
    sines = jnp.sin(colatitude)
    order_f = (first + jnp.arange(count, dtype=jnp.int32)).astype(jnp.float32)[:, None]
    factor_k = jnp.arange(1, MODES, dtype=jnp.int32).astype(jnp.float32)
    log_prod = jnp.concatenate([jnp.zeros((1,), jnp.float32), jnp.cumsum(jnp.log((2.0 * factor_k - 1.0) / (2.0 * factor_k)))])
    chosen = lax.dynamic_slice_in_dim(log_prod, first, count, 0)
    initial = jnp.exp(0.5 * jnp.log((2.0 * order_f + 1.0) / (4.0 * math.pi)) + 0.5 * chosen[:, None] + order_f * jnp.log(sines)[None, :])

    def advance(carry, degree_f):
        previous, earlier = carry
        scale_a = jnp.sqrt(jnp.maximum(4.0 * degree_f * degree_f - 1.0, 1.0) / jnp.maximum(degree_f * degree_f - order_f * order_f, 1.0))
        below = degree_f - 1.0
        scale_b = jnp.sqrt(jnp.maximum(below * below - order_f * order_f, 0.0) / jnp.maximum(4.0 * below * below - 1.0, 1.0))
        grown = scale_a * (cosines[None, :] * previous - scale_b * earlier)
        current = jnp.where(order_f == degree_f, initial, jnp.where(order_f < degree_f, grown, 0.0))
        return ((current, previous), current)
    zeros = jnp.zeros((count, NLAT), jnp.float32)
    degrees = jnp.arange(MODES, dtype=jnp.int32).astype(jnp.float32)
    _, table = lax.scan(advance, (zeros, zeros), degrees)
    weights = jnp.sqrt(2.0 * math.pi * math.pi * sines / NLAT)
    return jnp.transpose(table, (1, 0, 2)) * weights[None, None, :]

def fourier_table():
    columns = jnp.arange(NLON, dtype=jnp.int32)
    orders = jnp.arange(MODES, dtype=jnp.int32)
    phase = columns[:, None] * orders[None, :] % NLON
    angle = 2.0 * math.pi * phase.astype(jnp.float32) / NLON
    return jnp.concatenate([jnp.cos(angle), -jnp.sin(angle)], axis=1) * math.sqrt(2.0 / NLON)

def analysis(field, legendre, fourier):
    count = field.shape[0]
    spectra_lon = jnp.einsum('bjkc,kq->bjqc', field, fourier, precision=HIGHEST)
    spectra_lon = spectra_lon.reshape(count, NLAT, 2, MODES, WIDTH)
    return jnp.einsum('mlj,bjpmc->bpmlc', legendre, spectra_lon, precision=HIGHEST)

def synthesis(coeffs, legendre, fourier):
    count = coeffs.shape[0]
    columns = jnp.einsum('mlj,bpmlc->bjpmc', legendre, coeffs, precision=HIGHEST)
    columns = columns.reshape(count, NLAT, 2 * MODES, WIDTH)
    return jnp.einsum('bjqc,kq->bjkc', columns, fourier, precision=HIGHEST)

def gelu_tanh(values):
    return jax.nn.gelu(values, approximate=True)

def reference(inputs, saved, grad_out, w_up, w_down, w_filter):
    flat_grad = grad_out.reshape(-1, WIDTH)
    flat_saved = saved.reshape(-1, WIDTH)
    preact = jnp.dot(flat_saved, w_up, precision=HIGHEST, preferred_element_type=jnp.float32)
    activated, gelu_back = jax.vjp(gelu_tanh, preact)
    grad_act = jnp.dot(flat_grad, w_down.T, precision=HIGHEST, preferred_element_type=jnp.float32)
    grad_pre = gelu_back(grad_act)[0]
    grad_flat = flat_grad + jnp.dot(grad_pre, w_up.T, precision=HIGHEST, preferred_element_type=jnp.float32)
    point_scale = 1.0 / math.sqrt(SAMPLES * NLAT * NLON)
    grad_up = jnp.dot(flat_saved.T, grad_pre, precision=HIGHEST, preferred_element_type=jnp.float32) * point_scale
    grad_down = jnp.dot(activated.T, flat_grad, precision=HIGHEST, preferred_element_type=jnp.float32) * point_scale
    grad_field = grad_flat.reshape(grad_out.shape)
    legendre = legendre_table(0, MODES)
    fourier = fourier_table()
    spectra = analysis(inputs, legendre, fourier)
    grad_spec = analysis(grad_field, legendre, fourier)
    grad_coef = jnp.einsum('bpmld,lcd->bpmlc', grad_spec, w_filter, precision=HIGHEST)
    grad_filter = jnp.einsum('bpmlc,bpmld->lcd', spectra, grad_spec, precision=HIGHEST) / math.sqrt(2.0 * SAMPLES * MODES)
    grad_input = grad_field + synthesis(grad_coef, legendre, fourier)
    return (grad_input, grad_up, grad_down, grad_filter)
```

```python
import math

import jax
import jax.numpy as jnp
import numpy as np
from jax import lax
from jax.sharding import PartitionSpec as P

NLAT = 128
NLON = 256
MODES = 128
WIDTH = 384
SAMPLES = 1


HIGHEST = lax.Precision.HIGH


def legendre_values():
    theta = np.pi * (np.arange(NLAT) + 0.5) / NLAT
    cosines, sines = np.cos(theta), np.sin(theta)
    order = np.arange(MODES, dtype=np.float64)[:, None]
    k = np.arange(1, MODES, dtype=np.float64)
    log_prod = np.concatenate([[0.0], np.cumsum(np.log((2 * k - 1) / (2 * k)))])
    initial = np.exp(
        0.5 * np.log((2 * order + 1) / (4 * np.pi))
        + 0.5 * log_prod[:, None]
        + order * np.log(sines)[None, :]
    )
    previous = np.zeros((MODES, NLAT))
    earlier = np.zeros((MODES, NLAT))
    rows = []
    for degree in range(MODES):
        l = float(degree)
        a = np.sqrt(np.maximum(4 * l * l - 1, 1) / np.maximum(l * l - order * order, 1))
        b = np.sqrt(
            np.maximum((l - 1) ** 2 - order * order, 0) / np.maximum(4 * (l - 1) ** 2 - 1, 1)
        )
        grown = a * (cosines[None, :] * previous - b * earlier)
        current = np.where(order == l, initial, np.where(order < l, grown, 0.0))
        previous, earlier = current, previous
        rows.append(current)
    table = np.stack(rows, axis=1)
    return table * np.sqrt(2 * np.pi * np.pi * sines / NLAT)[None, None, :]


def fourier_values():
    phase = (np.arange(NLON)[:, None] * np.arange(MODES)[None, :]) % NLON
    angle = 2 * np.pi * phase / NLON
    return np.concatenate([np.cos(angle), -np.sin(angle)], axis=1) * np.sqrt(2.0 / NLON)


def gelu_tanh(values):
    return jax.nn.gelu(values, approximate=True)


def shards(inputs, saved, grad_out, w_up, w_down, w_filter):
    order_count = MODES // lax.axis_size("lat")
    legendre = lax.dynamic_slice_in_dim(
        jnp.asarray(legendre_values().astype(np.float32)),
        lax.axis_index("lat") * order_count,
        order_count,
        0,
    )
    fourier = jnp.asarray(fourier_values().astype(np.float32))

    def analysis(field):
        full_rows = lax.all_to_all(field, "lon", split_axis=3, concat_axis=2, tiled=True)
        spectra_lon = jnp.einsum("bjkc,kq->bcjq", full_rows, fourier, precision=HIGHEST)
        spectra_lon = spectra_lon.reshape(
            spectra_lon.shape[0], spectra_lon.shape[1], spectra_lon.shape[2], 2, MODES
        )
        by_order = lax.all_to_all(spectra_lon, "lat", split_axis=4, concat_axis=2, tiled=True)
        coeffs = jnp.einsum("mlj,bcjpm->bpmlc", legendre, by_order, precision=HIGHEST)
        return lax.all_to_all(coeffs, "lon", split_axis=3, concat_axis=4, tiled=True)

    spectra = analysis(inputs)
    flat_grad = grad_out.reshape(-1, WIDTH)
    flat_saved = saved.reshape(-1, WIDTH)
    preact = jnp.dot(flat_saved, w_up, precision=HIGHEST, preferred_element_type=jnp.float32)
    activated, gelu_back = jax.vjp(gelu_tanh, preact)
    grad_act = jnp.dot(flat_grad, w_down.T, precision=HIGHEST, preferred_element_type=jnp.float32)
    grad_pre = gelu_back(grad_act)[0]
    grad_flat = flat_grad + jnp.dot(
        grad_pre, w_up.T, precision=HIGHEST, preferred_element_type=jnp.float32
    )
    point_scale = 1.0 / math.sqrt(SAMPLES * NLAT * NLON)
    part_up = jnp.dot(flat_saved.T, grad_pre, precision=HIGHEST, preferred_element_type=jnp.float32)
    part_down = jnp.dot(
        activated.T, flat_grad, precision=HIGHEST, preferred_element_type=jnp.float32
    )
    summed_up, summed_down = (
        lax.psum_scatter(part_up, ("lat", "lon"), scatter_dimension=1, tiled=True),
        lax.psum_scatter(part_down, ("lat", "lon"), scatter_dimension=0, tiled=True),
    )
    grad_up = summed_up * point_scale
    grad_down = summed_down * point_scale
    grad_field = grad_flat.reshape(grad_out.shape)
    grad_spec = analysis(grad_field)
    grad_coef = jnp.einsum("bpmld,lcd->bpmlc", grad_spec, w_filter, precision=HIGHEST)
    filter_scale = 1.0 / math.sqrt(2.0 * SAMPLES * MODES)
    partial_filter = jnp.einsum("bpmlc,bpmld->lcd", spectra, grad_spec, precision=HIGHEST)
    grad_filter = (
        lax.psum_scatter(partial_filter, "lat", scatter_dimension=1, tiled=True) * filter_scale
    )
    all_degrees = lax.all_to_all(grad_coef, "lon", split_axis=4, concat_axis=3, tiled=True)
    columns = jnp.einsum("mlj,bpmlc->bcjpm", legendre, all_degrees, precision=HIGHEST)
    by_row = lax.all_to_all(columns, "lat", split_axis=2, concat_axis=4, tiled=True)
    by_row = by_row.reshape(by_row.shape[0], by_row.shape[1], by_row.shape[2], 2 * MODES)
    gridded = jnp.einsum("bcjq,kq->bjkc", by_row, fourier, precision=HIGHEST)
    grad_input = grad_field + lax.all_to_all(
        gridded, "lon", split_axis=2, concat_axis=3, tiled=True
    )
    return (grad_input, grad_up, grad_down, grad_filter)


def solution(mesh):
    in_specs = (
        P(None, "lat", "lon", None),
        P(None, "lat", "lon", None),
        P(None, "lat", "lon", None),
        P(),
        P(),
        P("lon", None, None),
    )
    out_specs = (
        P(None, "lat", "lon", None),
        P(None, ("lat", "lon")),
        P(("lat", "lon"), None),
        P("lon", "lat", None),
    )
    return jax.shard_map(shards, mesh=mesh, in_specs=in_specs, out_specs=out_specs, check_vma=False)
```

```python
import math

import jax
import jax.numpy as jnp
import numpy as np
from jax import lax
from jax.experimental import pallas as pl
from jax.experimental.pallas import tpu as pltpu
from jax.sharding import PartitionSpec as P

NLAT = 128
NLON = 256
MODES = 128
WIDTH = 384
HIDDEN = 768
SAMPLES = 1
NDEV = 128
LON = 16
LAT = 8
POINTS = 256
MESH = pl.DeviceIdType.MESH
F32 = jnp.float32
BF16 = jnp.bfloat16

NN = (((1,), (0,)), ((), ()))
NT = (((1,), (1,)), ((), ()))
TN = (((0,), (0,)), ((), ()))


def legendre_values():
    theta = np.pi * (np.arange(NLAT) + 0.5) / NLAT
    cosines, sines = np.cos(theta), np.sin(theta)
    order = np.arange(MODES, dtype=np.float64)[:, None]
    k = np.arange(1, MODES, dtype=np.float64)
    log_prod = np.concatenate([[0.0], np.cumsum(np.log((2 * k - 1) / (2 * k)))])
    initial = np.exp(
        0.5 * np.log((2 * order + 1) / (4 * np.pi))
        + 0.5 * log_prod[:, None]
        + order * np.log(sines)[None, :]
    )
    previous = np.zeros((MODES, NLAT))
    earlier = np.zeros((MODES, NLAT))
    rows = []
    for degree in range(MODES):
        l = float(degree)
        a = np.sqrt(np.maximum(4 * l * l - 1, 1) / np.maximum(l * l - order * order, 1))
        b = np.sqrt(
            np.maximum((l - 1) ** 2 - order * order, 0) / np.maximum(4 * (l - 1) ** 2 - 1, 1)
        )
        grown = a * (cosines[None, :] * previous - b * earlier)
        current = np.where(order == l, initial, np.where(order < l, grown, 0.0))
        previous, earlier = current, previous
        rows.append(current)
    table = np.stack(rows, axis=1)
    return table * np.sqrt(2 * np.pi * np.pi * sines / NLAT)[None, None, :]


def fourier_values():
    phase = (np.arange(NLON)[:, None] * np.arange(MODES)[None, :]) % NLON
    angle = 2 * np.pi * phase / NLON
    return np.concatenate([np.cos(angle), -np.sin(angle)], axis=1) * np.sqrt(2.0 / NLON)


def halves(table):
    table = np.asarray(table, np.float32)
    high = table.astype(jnp.bfloat16)
    low = (table - high.astype(np.float32)).astype(jnp.bfloat16)
    return high, low


def split(x):
    high = x.astype(BF16)
    return high, (x - high.astype(F32)).astype(BF16)


def dot3(a, b, dims):
    def dot(u, v):
        return lax.dot_general(u, v, dims, preferred_element_type=F32)

    return dot(a[0], b[0]) + (dot(a[0], b[1]) + dot(a[1], b[0]))


def exchange(tiles, lane):
    tiles = list(tiles)
    for bit in (1, 2, 4):
        upper = jnp.bitwise_and(lane, 16 * bit) != 0
        for s in range(8):
            if s & bit:
                continue
            lo, hi = tiles[s], tiles[s | bit]
            tiles[s] = jnp.where(upper, pltpu.roll(hi, 16 * bit, 1), lo)
            tiles[s | bit] = jnp.where(upper, hi, pltpu.roll(lo, 128 - 16 * bit, 1))
    return tiles


def kernel(
    x_hbm, saved_hbm, gout_hbm, up_hbm, down_hbm, filt_hbm, ta_hbm, ts_hbm, fo_hbm,
    gin_out, up_out, gf_out,
    x, saved, gout, up, down, filt, ta, ts, fo,
    send1, recv1, send2, recv2, send3, recv3, send4, recv4,
    act, gpre, field, part, pieces, pair, others, circle, zbuf, wbuf, spec, gfil, gfrecv, sums,
    load_sem, ssem, rsem, psem, osem, gsem, out_sem,
):
    lat = lax.axis_index("lat")
    lon = lax.axis_index("lon")
    me = lat * LON + lon
    degree = lon * LAT + lat
    core = lax.rem(lon, 2)
    chip = me // 2

    def by_place(d):
        return (d // LON, lax.rem(d, LON))

    def by_degree(d):
        return (lax.rem(d, LAT), d // LAT)

    barrier = pltpu.get_barrier_semaphore()

    def greet(s, carry):
        pl.semaphore_signal(
            barrier, inc=1, device_id=by_place(lax.rem(me + s, NDEV)), device_id_type=MESH
        )
        return carry

    lax.fori_loop(1, NDEV, greet, 0)

    pairs = [
        (x_hbm, x), (saved_hbm, saved), (up_hbm, up), (gout_hbm, gout), (down_hbm, down),
        (fo_hbm, fo), (ta_hbm, ta), (filt_hbm.at[lat], filt), (ts_hbm, ts),
    ]
    loads = [pltpu.make_async_copy(s, d, load_sem.at[i]) for i, (s, d) in enumerate(pairs)]
    for load in loads:
        load.start()

    def scatter(src, dst, n, where, mine, slot):
        def one(s, carry):
            d = lax.rem(mine + s, NDEV)
            pltpu.make_async_remote_copy(
                src_ref=src.at[d],
                dst_ref=dst.at[slot],
                send_sem=ssem.at[n],
                recv_sem=rsem.at[n],
                device_id=where(d),
                device_id_type=MESH,
            ).start()
            return carry

        lax.fori_loop(1, NDEV, one, 0)
        pltpu.make_async_copy(src.at[mine], dst.at[slot], rsem.at[n]).start()

    def arrived(dst, n):
        pltpu.make_async_copy(dst, dst, rsem.at[n]).wait()

    def sent(src, n):
        some = src.at[pl.ds(0, NDEV - 1)]
        pltpu.make_async_copy(some, some, ssem.at[n]).wait()

    lane = lax.broadcasted_iota(jnp.int32, (8, 128), 1)

    def to_channels(values, dst):
        for c in range(3):
            for h in range(2):
                block = values[h * 128 : h * 128 + 128, c * 128 : c * 128 + 128]
                dst[:, c * 2 + h, :] = block.T

    def regroup_in(src):
        for c in range(3):
            for h in range(2):
                for top in range(2):
                    tiles = [
                        src[pl.ds(top * 8 + s, 8, stride=16), c * 2 + h, :] for s in range(8)
                    ]
                    for s, tile in enumerate(exchange(tiles, lane)):
                        circle[top, pl.ds(c * 128 + h * 8 + s, 8, stride=16), :] = tile

    def regroup_out(dst):
        for c in range(3):
            for h in range(2):
                for top in range(2):
                    tiles = [
                        circle[top, pl.ds(c * 128 + h * 8 + s, 8, stride=16), :]
                        for s in range(8)
                    ]
                    for s, tile in enumerate(exchange(tiles, lane)):
                        dst[pl.ds(top * 8 + s, 8, stride=16), c * 2 + h, :] = tile

    def per_order(table):
        def eight(i, carry):
            for u in range(8):
                m = i * 8 + u
                z = zbuf[m]
                high = z.astype(BF16).astype(F32)
                rows = jnp.concatenate([high, z - high], axis=0).astype(BF16)
                r = lax.dot_general(rows, table[m], NN, preferred_element_type=F32)
                wbuf[m] = r[:8, :128] + (r[:8, 128:] + r[8:, :128])
            return carry

        lax.fori_loop(0, MODES // 8, eight, 0)

    def analysis(src, dst):
        regroup_in(src)
        fields = split(jnp.concatenate([circle[0], circle[1]], axis=1))
        for p in range(2):
            rows = (fo[0, p * 128 : p * 128 + 128], fo[1, p * 128 : p * 128 + 128])
            y = dot3(rows, fields, NT)
            for c in range(3):
                zbuf[:, p * 3 + c, :] = y[:, c * 128 : c * 128 + 128]
        per_order(ta)
        for c in range(3):
            for p in range(2):
                dst[:, c * 2 + p, :] = wbuf[:, p * 3 + c, :].T

    zbuf[...] = jnp.zeros_like(zbuf)
    loads[0].wait()
    to_channels(x, send1.at[0])
    pl.semaphore_wait(barrier, NDEV - 1)
    scatter(send1.at[0], recv1.at[0], 0, by_place, me, me)

    loads[1].wait()
    loads[2].wait()
    saved2 = split(saved[...])
    up2 = split(up[...])
    act[...] = dot3(saved2, up2, NN)
    loads[3].wait()
    loads[4].wait()
    gout2 = split(gout[...])
    gpre[...] = dot3(gout2, split(down[...]), NT)
    pre = act[...]
    scale = math.sqrt(2.0 / math.pi)
    square = pre * pre
    t = jnp.tanh(scale * (pre + 0.044715 * (square * pre)))
    half = 0.5 * (1.0 + t)
    act[...] = pre * half
    gpre[...] = gpre[...] * (
        half + (0.5 * scale) * pre * (1.0 - t * t) * (1.0 + (3.0 * 0.044715) * square)
    )
    field[...] = gout[...] + dot3(split(gpre[...]), up2, NT)
    to_channels(field, send1.at[1])
    scatter(send1.at[1], recv1.at[1], 1, by_place, me, me)

    def cut(first):
        for to in range(2):
            for k in range(6):
                for n in range(3):
                    pieces[to, :, n, first + k, :] = part[n, pl.ds(6 * to + k, 64, stride=12), :]

    def share_of(rows, columns, first):
        product = dot3(split(rows[...]), split(columns[...]), TN)
        for n in range(3):
            part[n] = product[:, n * 128 : n * 128 + 128]
        cut(first)

    share_of(gpre, saved, 0)
    share_of(act, gout, 6)
    partner = pltpu.make_async_remote_copy(
        src_ref=pieces.at[1 - core],
        dst_ref=pair,
        send_sem=psem.at[0],
        recv_sem=psem.at[1],
        device_id=(lat, lon + 1 - 2 * core),
        device_id_type=MESH,
    )
    partner.start()

    loads[5].wait()
    loads[6].wait()
    arrived(recv1.at[0], 0)
    analysis(recv1.at[0], send2.at[0])
    scatter(send2.at[0], recv2.at[0], 2, by_degree, degree, me)
    arrived(recv1.at[1], 1)
    analysis(recv1.at[1], send2.at[1])
    scatter(send2.at[1], recv2.at[1], 3, by_degree, degree, me)

    partner.wait()
    for n in range(3):
        for k in range(12):
            pair[:, n, k, :] = pair[:, n, k, :] + pieces[core, :, n, k, :]

    def owner(s, carry):
        d = lax.rem(chip + s, NDEV // 2)
        pltpu.make_async_remote_copy(
            src_ref=pair.at[d],
            dst_ref=others.at[chip],
            send_sem=osem.at[0],
            recv_sem=osem.at[1],
            device_id=by_place(2 * d + core),
            device_id_type=MESH,
        ).start()
        return carry

    lax.fori_loop(1, NDEV // 2, owner, 0)
    pltpu.make_async_copy(pair.at[chip], others.at[chip], osem.at[1]).start()

    loads[7].wait()
    arrived(recv2.at[1], 3)
    for c in range(3):
        for p in range(2):
            spec[1, c * 128 : c * 128 + 128, p * 128 : p * 128 + 128] = recv2[1, :, c * 2 + p, :]
    gspec2 = split(spec[1])
    coef = dot3(split(filt[...]), gspec2, NN)
    for c in range(3):
        for p in range(2):
            send3[:, c * 2 + p, :] = coef[c * 128 : c * 128 + 128, p * 128 : p * 128 + 128]
    scatter(send3, recv3, 4, by_place, me, degree)

    arrived(recv2.at[0], 2)
    for c in range(3):
        for p in range(2):
            spec[0, c * 128 : c * 128 + 128, p * 128 : p * 128 + 128] = recv2[0, :, c * 2 + p, :]
    gfil[...] = dot3(split(spec[0]), split(spec[1]), NT) * (
        1.0 / math.sqrt(2.0 * SAMPLES * MODES)
    )
    share = WIDTH // LAT

    def rows_of(d):
        return gfil.at[pl.ds(pl.multiple_of(d * share, 8), share)]

    def column(s, carry):
        d = lax.rem(lat + s, LAT)
        pltpu.make_async_remote_copy(
            src_ref=rows_of(d),
            dst_ref=gfrecv.at[lat],
            send_sem=gsem.at[0],
            recv_sem=gsem.at[1],
            device_id=(d, lon),
            device_id_type=MESH,
        ).start()
        return carry

    lax.fori_loop(1, LAT, column, 0)
    pltpu.make_async_copy(rows_of(lat), gfrecv.at[lat], gsem.at[1]).start()

    loads[8].wait()
    arrived(recv3, 4)
    for c in range(3):
        for p in range(2):
            zbuf[:, p * 3 + c, :] = recv3[:, c * 2 + p, :].T
    per_order(ts)
    for c in range(3):
        for p in range(2):
            spec[0, c * 128 : c * 128 + 128, p * 128 : p * 128 + 128] = wbuf[:, p * 3 + c, :].T
    grid = dot3(split(spec[0]), (fo[0], fo[1]), NN)
    circle[0] = grid[:, :128]
    circle[1] = grid[:, 128:]
    regroup_out(send4)
    scatter(send4, recv4, 5, by_place, me, me)

    pltpu.make_async_copy(others, others, osem.at[1]).wait()
    point_scale = 1.0 / math.sqrt(SAMPLES * NLAT * NLON)
    sums[...] = jnp.sum(others[...], axis=0) * point_scale
    pltpu.make_async_copy(gfrecv, gfrecv, gsem.at[1]).wait()
    stores = [
        pltpu.make_async_copy(sums, up_out, out_sem.at[0]),
        pltpu.make_async_copy(gfrecv, gf_out, out_sem.at[1]),
    ]
    for store in stores:
        store.start()

    arrived(recv4, 5)
    for c in range(3):
        for h in range(2):
            rows, lanes = slice(h * 128, h * 128 + 128), slice(c * 128, c * 128 + 128)
            field[rows, lanes] = field[rows, lanes] + recv4[:, c * 2 + h, :].T
    last = pltpu.make_async_copy(field, gin_out, out_sem.at[2])
    last.start()

    sent(send1.at[0], 0)
    sent(send1.at[1], 1)
    sent(send2.at[0], 2)
    sent(send2.at[1], 3)
    sent(send3, 4)
    sent(send4, 5)
    some = pair.at[pl.ds(0, NDEV // 2 - 1)]
    pltpu.make_async_copy(some, some, osem.at[0]).wait()
    some = gfil.at[pl.ds(0, WIDTH - share)]
    pltpu.make_async_copy(some, some, gsem.at[0]).wait()
    for store in stores:
        store.wait()
    last.wait()


def shards(inputs, saved, grad_out, w_up, w_down, w_filter):
    legendre = legendre_values()
    ta = np.concatenate(halves(legendre.transpose(0, 2, 1)), axis=2)
    ts = np.concatenate(halves(legendre), axis=2)
    fo = np.stack(halves(fourier_values().T))
    anywhere = pl.BlockSpec(memory_space=pl.ANY)

    def block():
        return pltpu.VMEM((NDEV, 6, 128), F32)

    def blocks(n):
        return pltpu.VMEM((n, NDEV, 6, 128), F32)

    gin, sums, gfil = pl.pallas_call(
        kernel,
        out_shape=(
            jax.ShapeDtypeStruct((POINTS, WIDTH), F32),
            jax.ShapeDtypeStruct((3, 12, 128), F32),
            jax.ShapeDtypeStruct((LAT, WIDTH // LAT, WIDTH), F32),
        ),
        in_specs=[anywhere] * 9,
        out_specs=(anywhere,) * 3,
        scratch_shapes=[
            pltpu.VMEM((POINTS, WIDTH), F32),
            pltpu.VMEM((POINTS, WIDTH), F32),
            pltpu.VMEM((POINTS, WIDTH), F32),
            pltpu.VMEM((WIDTH, HIDDEN), F32),
            pltpu.VMEM((HIDDEN, WIDTH), F32),
            pltpu.VMEM((WIDTH, WIDTH), F32),
            pltpu.VMEM((MODES, NLAT, 256), BF16),
            pltpu.VMEM((MODES, MODES, 256), BF16),
            pltpu.VMEM((2, 256, 256), BF16),
            blocks(2), blocks(2), blocks(2), blocks(2), block(), block(), block(), block(),
            pltpu.VMEM((POINTS, HIDDEN), F32),
            pltpu.VMEM((POINTS, HIDDEN), F32),
            pltpu.VMEM((POINTS, WIDTH), F32),
            pltpu.VMEM((3, HIDDEN, 128), F32),
            pltpu.VMEM((2, NDEV // 2, 3, 12, 128), F32),
            pltpu.VMEM((NDEV // 2, 3, 12, 128), F32),
            pltpu.VMEM((NDEV // 2, 3, 12, 128), F32),
            pltpu.VMEM((2, WIDTH, 128), F32),
            pltpu.VMEM((MODES, 8, 128), F32),
            pltpu.VMEM((MODES, 8, 128), F32),
            pltpu.VMEM((2, WIDTH, 256), F32),
            pltpu.VMEM((WIDTH, WIDTH), F32),
            pltpu.VMEM((LAT, WIDTH // LAT, WIDTH), F32),
            pltpu.VMEM((3, 12, 128), F32),
            pltpu.SemaphoreType.DMA((9,)),
            pltpu.SemaphoreType.DMA((6,)),
            pltpu.SemaphoreType.DMA((6,)),
            pltpu.SemaphoreType.DMA((2,)),
            pltpu.SemaphoreType.DMA((2,)),
            pltpu.SemaphoreType.DMA((2,)),
            pltpu.SemaphoreType.DMA((3,)),
        ],
        compiler_params=pltpu.CompilerParams(
            collective_id=0, has_side_effects=True, vmem_limit_bytes=56 << 20
        ),
    )(
        inputs.reshape(POINTS, WIDTH), saved.reshape(POINTS, WIDTH),
        grad_out.reshape(POINTS, WIDTH), w_up, w_down, w_filter,
        jnp.asarray(ta), jnp.asarray(ts), jnp.asarray(fo),
    )
    sums = sums.transpose(1, 0, 2).reshape(12, WIDTH)
    return (gin.reshape(inputs.shape), sums[:6].T, sums[6:], gfil)


def solution(mesh):
    in_specs = (
        P(None, "lat", "lon", None),
        P(None, "lat", "lon", None),
        P(None, "lat", "lon", None),
        P(),
        P(),
        P("lon", None, None),
    )
    out_specs = (
        P(None, "lat", "lon", None),
        P(None, ("lat", "lon")),
        P(("lat", "lon"), None),
        P("lon", "lat", None),
    )
    return jax.shard_map(shards, mesh=mesh, in_specs=in_specs, out_specs=out_specs, check_vma=False)
```

```python
import math

import jax
import jax.numpy as jnp
import numpy as np
from jax import lax
from jax.experimental import pallas as pl
from jax.experimental.pallas import tpu as pltpu
from jax.sharding import PartitionSpec as P

NLAT = 128
NLON = 256
MODES = 128
WIDTH = 384
HIDDEN = 768
SAMPLES = 1
NDEV = 128
LON = 16
LAT = 8
POINTS = 256
EARLY = 2
AWAY = (0, 1, 2, 1)
STEPS = sorted(
    [(i // 32, i // 8 % 4, i // 2 % 4, i % 2) for i in range(1, NDEV)],
    key=lambda step: -sum(AWAY[k] for k in step[:3]),
)
MESH = pl.DeviceIdType.MESH
F32 = jnp.float32
BF16 = jnp.bfloat16

NN = (((1,), (0,)), ((), ()))
NT = (((1,), (1,)), ((), ()))
TN = (((0,), (0,)), ((), ()))


def legendre_values():
    theta = np.pi * (np.arange(NLAT) + 0.5) / NLAT
    cosines, sines = np.cos(theta), np.sin(theta)
    order = np.arange(MODES, dtype=np.float64)[:, None]
    k = np.arange(1, MODES, dtype=np.float64)
    log_prod = np.concatenate([[0.0], np.cumsum(np.log((2 * k - 1) / (2 * k)))])
    initial = np.exp(
        0.5 * np.log((2 * order + 1) / (4 * np.pi))
        + 0.5 * log_prod[:, None]
        + order * np.log(sines)[None, :]
    )
    previous = np.zeros((MODES, NLAT))
    earlier = np.zeros((MODES, NLAT))
    rows = []
    for degree in range(MODES):
        l = float(degree)
        a = np.sqrt(np.maximum(4 * l * l - 1, 1) / np.maximum(l * l - order * order, 1))
        b = np.sqrt(
            np.maximum((l - 1) ** 2 - order * order, 0) / np.maximum(4 * (l - 1) ** 2 - 1, 1)
        )
        grown = a * (cosines[None, :] * previous - b * earlier)
        current = np.where(order == l, initial, np.where(order < l, grown, 0.0))
        previous, earlier = current, previous
        rows.append(current)
    table = np.stack(rows, axis=1)
    return table * np.sqrt(2 * np.pi * np.pi * sines / NLAT)[None, None, :]


def fourier_values():
    phase = (np.arange(NLON)[:, None] * np.arange(MODES)[None, :]) % NLON
    angle = 2 * np.pi * phase / NLON
    return np.concatenate([np.cos(angle), -np.sin(angle)], axis=1) * np.sqrt(2.0 / NLON)


def halves(table):
    table = np.asarray(table, np.float32)
    high = table.astype(jnp.bfloat16)
    low = (table - high.astype(np.float32)).astype(jnp.bfloat16)
    return high, low


def split(x):
    high = x.astype(BF16)
    return high, (x - high.astype(F32)).astype(BF16)


def dot3(a, b, dims):
    def dot(u, v):
        return lax.dot_general(u, v, dims, preferred_element_type=F32)

    return dot(a[0], b[0]) + (dot(a[0], b[1]) + dot(a[1], b[0]))


def exchange(tiles, lane):
    tiles = list(tiles)
    for bit in (1, 2, 4):
        upper = jnp.bitwise_and(lane, 16 * bit) != 0
        for s in range(8):
            if s & bit:
                continue
            lo, hi = tiles[s], tiles[s | bit]
            tiles[s] = jnp.where(upper, pltpu.roll(hi, 16 * bit, 1), lo)
            tiles[s | bit] = jnp.where(upper, hi, pltpu.roll(lo, 128 - 16 * bit, 1))
    return tiles


def kernel(
    x_hbm, saved_hbm, gout_hbm, up_hbm, down_hbm, filt_hbm, ta_hbm, ts_hbm, fo_hbm,
    gin_out, up_out, gf_out,
    x, saved, gout, up, down, filt, ta, ts, fo,
    send1, recv1, send2, recv2, send3, recv3, send4, recv4,
    act, gpre, field, part, pieces, pair, others, circle, zbuf, wbuf, spec, gfil, gfrecv, sums,
    load_sem, ssem, rsem, psem, osem, gsem, out_sem,
):
    lat = lax.axis_index("lat")
    lon = lax.axis_index("lon")
    me = lat * LON + lon
    core = lax.rem(lon, 2)
    chip = me // 2

    def by_place(d):
        return (d // LON, lax.rem(d, LON))

    x_at, y_lo = lax.rem(lat, 4), lat // 4
    z_at, y_hi = lax.rem(lon // 2, 4), lon // 8
    y_at = y_hi * 2 + y_lo
    ys = [lax.rem(y_at + i, 4) for i in range(4)]
    lats = [[lax.rem(y, 2) * 4 + lax.rem(x_at + i, 4) for i in range(4)] for y in ys]
    lons = [
        [
            [(y // 2) * 8 + lax.rem(z_at + i, 4) * 2 + lax.rem(core + c, 2) for c in range(2)]
            for i in range(4)
        ]
        for y in ys
    ]

    barrier = pltpu.get_barrier_semaphore()

    def greet(s, carry):
        pl.semaphore_signal(
            barrier, inc=1, device_id=by_place(lax.rem(me + s, NDEV)), device_id_type=MESH
        )
        return carry

    lax.fori_loop(1, NDEV, greet, 0)

    pairs = [
        (saved_hbm, saved), (up_hbm, up), (gout_hbm, gout), (down_hbm, down), (x_hbm, x),
        (fo_hbm, fo), (ta_hbm, ta), (filt_hbm.at[lat], filt), (ts_hbm, ts),
    ]
    loads = [pltpu.make_async_copy(s, d, load_sem.at[i]) for i, (s, d) in enumerate(pairs)]
    for load in loads:
        load.start()

    def scatter(src, dst, n):
        for y, x_, z, c in STEPS:
            to_lat = lats[y][x_]
            to_lon = lons[y][z][c]
            pltpu.make_async_remote_copy(
                src_ref=src.at[to_lat * LON + to_lon],
                dst_ref=dst.at[me],
                send_sem=ssem.at[n],
                recv_sem=rsem.at[n],
                device_id=(to_lat, to_lon),
                device_id_type=MESH,
            ).start()
        pltpu.make_async_copy(src.at[me], dst.at[me], rsem.at[n]).start()

    def arrived(dst, n):
        pltpu.make_async_copy(dst, dst, rsem.at[n]).wait()

    def sent(src, n):
        some = src.at[pl.ds(0, NDEV - 1)]
        pltpu.make_async_copy(some, some, ssem.at[n]).wait()

    lane = lax.broadcasted_iota(jnp.int32, (8, 128), 1)

    def to_channels(values, dst):
        for c in range(3):
            for h in range(2):
                block = values[h * 128 : h * 128 + 128, c * 128 : c * 128 + 128]
                dst[:, c * 2 + h, :] = block.T

    def regroup_in(src):
        for c in range(3):
            for h in range(2):
                for top in range(2):
                    tiles = [
                        src[pl.ds(top * 8 + s, 8, stride=16), c * 2 + h, :] for s in range(8)
                    ]
                    for s, tile in enumerate(exchange(tiles, lane)):
                        circle[top, pl.ds(c * 128 + h * 8 + s, 8, stride=16), :] = tile

    def regroup_out(dst):
        for c in range(3):
            for h in range(2):
                for top in range(2):
                    tiles = [
                        circle[top, pl.ds(c * 128 + h * 8 + s, 8, stride=16), :]
                        for s in range(8)
                    ]
                    for s, tile in enumerate(exchange(tiles, lane)):
                        dst[pl.ds(top * 8 + s, 8, stride=16), c * 2 + h, :] = tile

    def per_order(table):
        def eight(i, carry):
            for u in range(8):
                m = i * 8 + u
                z = zbuf[m]
                high = z.astype(BF16).astype(F32)
                rows = jnp.concatenate([high, z - high], axis=0).astype(BF16)
                r = lax.dot_general(rows, table[m], NN, preferred_element_type=F32)
                wbuf[m] = r[:8, :128] + (r[:8, 128:] + r[8:, :128])
            return carry

        lax.fori_loop(0, MODES // 8, eight, 0)

    def analysis(src, dst):
        regroup_in(src)
        fields = split(jnp.concatenate([circle[0], circle[1]], axis=1))
        for p in range(2):
            rows = (fo[0, p * 128 : p * 128 + 128], fo[1, p * 128 : p * 128 + 128])
            y = dot3(rows, fields, NT)
            for c in range(3):
                zbuf[:, p * 3 + c, :] = y[:, c * 128 : c * 128 + 128]
        per_order(ta)
        for c in range(3):
            for p in range(2):
                dst[:, c * 2 + p, :] = wbuf[:, p * 3 + c, :].T

    loads[0].wait()
    loads[1].wait()
    saved2 = split(saved[...])
    up2 = split(up[...])
    act[...] = dot3(saved2, up2, NN)
    loads[2].wait()
    loads[3].wait()
    gout2 = split(gout[...])
    gpre[...] = dot3(gout2, split(down[...]), NT)
    pre = act[...]
    scale = math.sqrt(2.0 / math.pi)
    square = pre * pre
    t = jnp.tanh(scale * (pre + 0.044715 * (square * pre)))
    half = 0.5 * (1.0 + t)
    act[...] = pre * half
    gpre[...] = gpre[...] * (
        half + (0.5 * scale) * pre * (1.0 - t * t) * (1.0 + (3.0 * 0.044715) * square)
    )
    field[...] = gout[...] + dot3(split(gpre[...]), up2, NT)
    to_channels(field, send1.at[1])
    pl.semaphore_wait(barrier, NDEV - 1)
    scatter(send1.at[1], recv1.at[1], 1)

    loads[4].wait()
    to_channels(x, send1.at[0])
    scatter(send1.at[0], recv1.at[0], 0)
    zbuf[...] = jnp.zeros_like(zbuf)

    def cut(first):
        for to in range(2):
            for k in range(6):
                for n in range(3):
                    pieces[to, :, n, first + k, :] = part[n, pl.ds(6 * to + k, 64, stride=12), :]

    def share_of(rows, columns, first):
        product = dot3(split(rows[...]), split(columns[...]), TN)
        for n in range(3):
            part[n] = product[:, n * 128 : n * 128 + 128]
        cut(first)

    share_of(gpre, saved, 0)
    share_of(act, gout, 6)
    partner = pltpu.make_async_remote_copy(
        src_ref=pieces.at[1 - core],
        dst_ref=pair,
        send_sem=psem.at[0],
        recv_sem=psem.at[1],
        device_id=(lat, lon + 1 - 2 * core),
        device_id_type=MESH,
    )
    partner.start()

    loads[5].wait()
    loads[6].wait()
    arrived(recv1.at[1], 1)
    analysis(recv1.at[1], send2.at[1])
    scatter(send2.at[1], recv2.at[1], 3)

    partner.wait()
    pair[...] = pair[...] + pieces[core]

    def owner(s, carry):
        d = lax.rem(chip + s, NDEV // 2)
        pltpu.make_async_remote_copy(
            src_ref=pair.at[d],
            dst_ref=others.at[chip],
            send_sem=osem.at[0],
            recv_sem=osem.at[1],
            device_id=by_place(2 * d + core),
            device_id_type=MESH,
        ).start()
        return carry

    lax.fori_loop(1, EARLY, owner, 0)
    pltpu.make_async_copy(pair.at[chip], others.at[chip], osem.at[1]).start()

    arrived(recv1.at[0], 0)
    analysis(recv1.at[0], send2.at[0])
    scatter(send2.at[0], recv2.at[0], 2)

    loads[7].wait()
    arrived(recv2.at[1], 3)
    for c in range(3):
        for p in range(2):
            spec[1, c * 128 : c * 128 + 128, p * 128 : p * 128 + 128] = recv2[1, :, c * 2 + p, :]
    gspec2 = split(spec[1])
    coef = dot3(split(filt[...]), gspec2, NN)
    for c in range(3):
        for p in range(2):
            send3[:, c * 2 + p, :] = coef[c * 128 : c * 128 + 128, p * 128 : p * 128 + 128]
    scatter(send3, recv3, 4)

    arrived(recv2.at[0], 2)
    for c in range(3):
        for p in range(2):
            spec[0, c * 128 : c * 128 + 128, p * 128 : p * 128 + 128] = recv2[0, :, c * 2 + p, :]
    gfil[...] = dot3(split(spec[0]), split(spec[1]), NT) * (
        1.0 / math.sqrt(2.0 * SAMPLES * MODES)
    )
    share = WIDTH // LAT

    def rows_of(d):
        return gfil.at[pl.ds(pl.multiple_of(d * share, 8), share)]

    def column(s, carry):
        d = lax.rem(lat + s, LAT)
        pltpu.make_async_remote_copy(
            src_ref=rows_of(d),
            dst_ref=gfrecv.at[lat],
            send_sem=gsem.at[0],
            recv_sem=gsem.at[1],
            device_id=(d, lon),
            device_id_type=MESH,
        ).start()
        return carry

    lax.fori_loop(1, LAT, column, 0)
    pltpu.make_async_copy(rows_of(lat), gfrecv.at[lat], gsem.at[1]).start()
    lax.fori_loop(EARLY, NDEV // 2, owner, 0)

    loads[8].wait()
    arrived(recv3, 4)
    for c in range(3):
        for p in range(2):
            zbuf[:, p * 3 + c, :] = recv3[:, c * 2 + p, :].T
    per_order(ts)
    for c in range(3):
        for p in range(2):
            spec[0, c * 128 : c * 128 + 128, p * 128 : p * 128 + 128] = wbuf[:, p * 3 + c, :].T
    grid = dot3(split(spec[0]), (fo[0], fo[1]), NN)
    circle[0] = grid[:, :128]
    circle[1] = grid[:, 128:]
    regroup_out(send4)
    scatter(send4, recv4, 5)

    pltpu.make_async_copy(others, others, osem.at[1]).wait()
    point_scale = 1.0 / math.sqrt(SAMPLES * NLAT * NLON)
    total = jnp.sum(others[...], axis=0) * point_scale
    for n in range(3):
        sums[0, :, n * 128 : n * 128 + 128] = total[n, :6]
        sums[1, :, n * 128 : n * 128 + 128] = total[n, 6:]
    pltpu.make_async_copy(gfrecv, gfrecv, gsem.at[1]).wait()
    stores = [
        pltpu.make_async_copy(sums, up_out, out_sem.at[0]),
        pltpu.make_async_copy(gfrecv, gf_out, out_sem.at[1]),
    ]
    for store in stores:
        store.start()

    arrived(recv4, 5)
    for c in range(3):
        for h in range(2):
            rows, lanes = slice(h * 128, h * 128 + 128), slice(c * 128, c * 128 + 128)
            field[rows, lanes] = field[rows, lanes] + recv4[:, c * 2 + h, :].T
    last = pltpu.make_async_copy(field, gin_out, out_sem.at[2])
    last.start()

    sent(send1.at[0], 0)
    sent(send1.at[1], 1)
    sent(send2.at[0], 2)
    sent(send2.at[1], 3)
    sent(send3, 4)
    sent(send4, 5)
    some = pair.at[pl.ds(0, NDEV // 2 - 1)]
    pltpu.make_async_copy(some, some, osem.at[0]).wait()
    some = gfil.at[pl.ds(0, WIDTH - share)]
    pltpu.make_async_copy(some, some, gsem.at[0]).wait()
    for store in stores:
        store.wait()
    last.wait()


def results(gin, sums, gfil, gin_out, up_out, down_out, gfil_out, a, b, c, sem, out_sem):
    loads = [
        pltpu.make_async_copy(gfil, c, sem.at[0]),
        pltpu.make_async_copy(gin, a, sem.at[1]),
        pltpu.make_async_copy(sums, b, sem.at[2]),
    ]
    pairs = [(c, gfil_out), (a, gin_out), (b.at[0], up_out), (b.at[1], down_out)]
    stores = [pltpu.make_async_copy(s, d, out_sem.at[i]) for i, (s, d) in enumerate(pairs)]
    for load in loads:
        load.start()
    for i, store in enumerate(stores):
        if i < 3:
            loads[i].wait()
        store.start()
    for store in stores:
        store.wait()


def shards(inputs, saved, grad_out, w_up, w_down, w_filter):
    legendre = legendre_values()
    device = np.arange(NDEV)
    legendre = legendre[:, (device % LON) * LAT + device // LON]
    ta = np.concatenate(halves(legendre.transpose(0, 2, 1)), axis=2)
    ts = np.concatenate(halves(legendre), axis=2)
    fo = np.stack(halves(fourier_values().T))
    anywhere = pl.BlockSpec(memory_space=pl.ANY)

    def block():
        return pltpu.VMEM((NDEV, 6, 128), F32)

    def blocks(n):
        return pltpu.VMEM((n, NDEV, 6, 128), F32)

    gin, sums, gfil = pl.pallas_call(
        kernel,
        out_shape=(
            jax.ShapeDtypeStruct((POINTS, WIDTH), F32),
            jax.ShapeDtypeStruct((2, 6, WIDTH), F32),
            jax.ShapeDtypeStruct((LAT, WIDTH // LAT, WIDTH), F32),
        ),
        in_specs=[anywhere] * 9,
        out_specs=(anywhere,) * 3,
        scratch_shapes=[
            pltpu.VMEM((POINTS, WIDTH), F32),
            pltpu.VMEM((POINTS, WIDTH), F32),
            pltpu.VMEM((POINTS, WIDTH), F32),
            pltpu.VMEM((WIDTH, HIDDEN), F32),
            pltpu.VMEM((HIDDEN, WIDTH), F32),
            pltpu.VMEM((WIDTH, WIDTH), F32),
            pltpu.VMEM((MODES, NLAT, 256), BF16),
            pltpu.VMEM((MODES, MODES, 256), BF16),
            pltpu.VMEM((2, 256, 256), BF16),
            blocks(2), blocks(2), blocks(2), blocks(2), block(), block(), block(), block(),
            pltpu.VMEM((POINTS, HIDDEN), F32),
            pltpu.VMEM((POINTS, HIDDEN), F32),
            pltpu.VMEM((POINTS, WIDTH), F32),
            pltpu.VMEM((3, HIDDEN, 128), F32),
            pltpu.VMEM((2, NDEV // 2, 3, 12, 128), F32),
            pltpu.VMEM((NDEV // 2, 3, 12, 128), F32),
            pltpu.VMEM((NDEV // 2, 3, 12, 128), F32),
            pltpu.VMEM((2, WIDTH, 128), F32),
            pltpu.VMEM((MODES, 8, 128), F32),
            pltpu.VMEM((MODES, 8, 128), F32),
            pltpu.VMEM((2, WIDTH, 256), F32),
            pltpu.VMEM((WIDTH, WIDTH), F32),
            pltpu.VMEM((LAT, WIDTH // LAT, WIDTH), F32),
            pltpu.VMEM((2, 6, WIDTH), F32),
            pltpu.SemaphoreType.DMA((9,)),
            pltpu.SemaphoreType.DMA((6,)),
            pltpu.SemaphoreType.DMA((6,)),
            pltpu.SemaphoreType.DMA((2,)),
            pltpu.SemaphoreType.DMA((2,)),
            pltpu.SemaphoreType.DMA((2,)),
            pltpu.SemaphoreType.DMA((3,)),
        ],
        compiler_params=pltpu.CompilerParams(
            collective_id=0, has_side_effects=True, vmem_limit_bytes=56 << 20
        ),
    )(
        inputs.reshape(POINTS, WIDTH), saved.reshape(POINTS, WIDTH),
        grad_out.reshape(POINTS, WIDTH), w_up, w_down, w_filter,
        jnp.asarray(ta), jnp.asarray(ts), jnp.asarray(fo),
    )
    gin, up, down, gfil = pl.pallas_call(
        results,
        out_shape=(
            jax.ShapeDtypeStruct((POINTS, WIDTH), F32),
            jax.ShapeDtypeStruct((6, WIDTH), F32),
            jax.ShapeDtypeStruct((6, WIDTH), F32),
            jax.ShapeDtypeStruct((LAT, WIDTH // LAT, WIDTH), F32),
        ),
        in_specs=[anywhere] * 3,
        out_specs=(anywhere,) * 4,
        scratch_shapes=[
            pltpu.VMEM((POINTS, WIDTH), F32),
            pltpu.VMEM((2, 6, WIDTH), F32),
            pltpu.VMEM((LAT, WIDTH // LAT, WIDTH), F32),
            pltpu.SemaphoreType.DMA((3,)),
            pltpu.SemaphoreType.DMA((4,)),
        ],
    )(gin, sums, gfil)
    return (gin.reshape(inputs.shape), up.T, down, gfil)


def solution(mesh):
    in_specs = (
        P(None, "lat", "lon", None),
        P(None, "lat", "lon", None),
        P(None, "lat", "lon", None),
        P(),
        P(),
        P("lon", None, None),
    )
    out_specs = (
        P(None, "lat", "lon", None),
        P(None, ("lat", "lon")),
        P(("lat", "lon"), None),
        P("lon", "lat", None),
    )
    return jax.shard_map(shards, mesh=mesh, in_specs=in_specs, out_specs=out_specs, check_vma=False)
```

```python
import math

import jax
import jax.numpy as jnp
import numpy as np
from jax import lax
from jax.experimental import pallas as pl
from jax.experimental.pallas import tpu as pltpu
from jax.sharding import PartitionSpec as P

NLAT = 128
NLON = 256
MODES = 128
WIDTH = 384
HIDDEN = 768
SAMPLES = 1
NDEV = 128
LON = 16
LAT = 8
POINTS = 256
BLOCK = 32
AWAY = (0, 1, 2, 1)
STEPS = sorted(
    [(i // 32, i // 8 % 4, i // 2 % 4, i % 2) for i in range(1, NDEV)],
    key=lambda step: -sum(AWAY[k] for k in step[:3]),
)
MESH = pl.DeviceIdType.MESH
F32 = jnp.float32
BF16 = jnp.bfloat16

NN = (((1,), (0,)), ((), ()))
NT = (((1,), (1,)), ((), ()))
TN = (((0,), (0,)), ((), ()))


def legendre_values():
    theta = np.pi * (np.arange(NLAT) + 0.5) / NLAT
    cosines, sines = np.cos(theta), np.sin(theta)
    order = np.arange(MODES, dtype=np.float64)[:, None]
    k = np.arange(1, MODES, dtype=np.float64)
    log_prod = np.concatenate([[0.0], np.cumsum(np.log((2 * k - 1) / (2 * k)))])
    initial = np.exp(
        0.5 * np.log((2 * order + 1) / (4 * np.pi))
        + 0.5 * log_prod[:, None]
        + order * np.log(sines)[None, :]
    )
    previous = np.zeros((MODES, NLAT))
    earlier = np.zeros((MODES, NLAT))
    rows = []
    for degree in range(MODES):
        l = float(degree)
        a = np.sqrt(np.maximum(4 * l * l - 1, 1) / np.maximum(l * l - order * order, 1))
        b = np.sqrt(
            np.maximum((l - 1) ** 2 - order * order, 0) / np.maximum(4 * (l - 1) ** 2 - 1, 1)
        )
        grown = a * (cosines[None, :] * previous - b * earlier)
        current = np.where(order == l, initial, np.where(order < l, grown, 0.0))
        previous, earlier = current, previous
        rows.append(current)
    table = np.stack(rows, axis=1)
    return table * np.sqrt(2 * np.pi * np.pi * sines / NLAT)[None, None, :]


def fourier_values():
    phase = (np.arange(NLON)[:, None] * np.arange(MODES)[None, :]) % NLON
    angle = 2 * np.pi * phase / NLON
    return np.concatenate([np.cos(angle), -np.sin(angle)], axis=1) * np.sqrt(2.0 / NLON)


def halves(table):
    table = np.asarray(table, np.float32)
    high = table.astype(jnp.bfloat16)
    low = (table - high.astype(np.float32)).astype(jnp.bfloat16)
    return high, low


def split(x):
    high = x.astype(BF16)
    return high, (x - high.astype(F32)).astype(BF16)


def dot3(a, b, dims):
    def dot(u, v):
        return lax.dot_general(u, v, dims, preferred_element_type=F32)

    return dot(a[0], b[0]) + (dot(a[0], b[1]) + dot(a[1], b[0]))


def exchange(tiles, lane):
    tiles = list(tiles)
    for bit in (1, 2, 4):
        upper = jnp.bitwise_and(lane, 16 * bit) != 0
        for s in range(8):
            if s & bit:
                continue
            lo, hi = tiles[s], tiles[s | bit]
            tiles[s] = jnp.where(upper, pltpu.roll(hi, 16 * bit, 1), lo)
            tiles[s | bit] = jnp.where(upper, hi, pltpu.roll(lo, 128 - 16 * bit, 1))
    return tiles


def kernel(
    x_hbm, saved_hbm, gout_hbm, up_hbm, down_hbm, filt_hbm, ta_hbm, ts_hbm, fo_hbm,
    gin_out, up_out, gf_out,
    x, saved, gout, up, down, filt, ta, ts, fo,
    send1, recv1, send2, recv2, send3, recv3, send4, recv4,
    act, gpre, field, part, pieces, pair, ring, mid, others, circle, zbuf, wbuf, spec, gfil, gfrecv, sums,
    load_sem, ssem, rsem, psem, osem, gsem, out_sem,
):
    lat = lax.axis_index("lat")
    lon = lax.axis_index("lon")
    me = lat * LON + lon
    core = lax.rem(lon, 2)

    def by_place(d):
        return (d // LON, lax.rem(d, LON))

    x_at, y_lo = lax.rem(lat, 4), lat // 4
    z_at, y_hi = lax.rem(lon // 2, 4), lon // 8
    y_at = y_hi * 2 + y_lo
    ys = [lax.rem(y_at + i, 4) for i in range(4)]
    lats = [[lax.rem(y, 2) * 4 + lax.rem(x_at + i, 4) for i in range(4)] for y in ys]
    lons = [
        [
            [(y // 2) * 8 + lax.rem(z_at + i, 4) * 2 + lax.rem(core + c, 2) for c in range(2)]
            for i in range(4)
        ]
        for y in ys
    ]

    barrier = pltpu.get_barrier_semaphore()

    def greet(s, carry):
        pl.semaphore_signal(
            barrier, inc=1, device_id=by_place(lax.rem(me + s, NDEV)), device_id_type=MESH
        )
        return carry

    lax.fori_loop(1, NDEV, greet, 0)

    pairs = [
        (saved_hbm, saved), (up_hbm, up), (gout_hbm, gout), (down_hbm, down), (x_hbm, x),
        (fo_hbm, fo), (ta_hbm, ta), (filt_hbm.at[lat], filt), (ts_hbm, ts),
    ]
    loads = [pltpu.make_async_copy(s, d, load_sem.at[i]) for i, (s, d) in enumerate(pairs)]
    for load in loads:
        load.start()

    def scatter(src, dst, n):
        for y, x_, z, c in STEPS:
            to_lat = lats[y][x_]
            to_lon = lons[y][z][c]
            pltpu.make_async_remote_copy(
                src_ref=src.at[to_lat * LON + to_lon],
                dst_ref=dst.at[me],
                send_sem=ssem.at[n],
                recv_sem=rsem.at[n],
                device_id=(to_lat, to_lon),
                device_id_type=MESH,
            ).start()
        pltpu.make_async_copy(src.at[me], dst.at[me], rsem.at[n]).start()

    def arrived(dst, n):
        pltpu.make_async_copy(dst, dst, rsem.at[n]).wait()

    def sent(src, n):
        some = src.at[pl.ds(0, NDEV - 1)]
        pltpu.make_async_copy(some, some, ssem.at[n]).wait()

    lane = lax.broadcasted_iota(jnp.int32, (8, 128), 1)

    def to_channels(values, dst):
        for c in range(3):
            for h in range(2):
                block = values[h * 128 : h * 128 + 128, c * 128 : c * 128 + 128]
                dst[:, c * 2 + h, :] = block.T

    def regroup_in(src):
        for c in range(3):
            for h in range(2):
                for top in range(2):
                    tiles = [
                        src[pl.ds(top * 8 + s, 8, stride=16), c * 2 + h, :] for s in range(8)
                    ]
                    for s, tile in enumerate(exchange(tiles, lane)):
                        circle[top, pl.ds(c * 128 + h * 8 + s, 8, stride=16), :] = tile

    def regroup_out(dst):
        for c in range(3):
            for h in range(2):
                for top in range(2):
                    tiles = [
                        circle[top, pl.ds(c * 128 + h * 8 + s, 8, stride=16), :]
                        for s in range(8)
                    ]
                    for s, tile in enumerate(exchange(tiles, lane)):
                        dst[pl.ds(top * 8 + s, 8, stride=16), c * 2 + h, :] = tile

    def per_order(table):
        def several(i, carry):
            for u in range(BLOCK):
                m = i * BLOCK + u
                z = zbuf[m]
                high = z.astype(BF16).astype(F32)
                rows = jnp.concatenate([high, z - high], axis=0).astype(BF16)
                r = lax.dot_general(rows, table[m], NN, preferred_element_type=F32)
                wbuf[m] = r[:8, :128] + (r[:8, 128:] + r[8:, :128])
            return carry

        lax.fori_loop(0, MODES // BLOCK, several, 0)

    def analysis(src, dst):
        regroup_in(src)
        fields = split(jnp.concatenate([circle[0], circle[1]], axis=1))
        for p in range(2):
            rows = (fo[0, p * 128 : p * 128 + 128], fo[1, p * 128 : p * 128 + 128])
            y = dot3(rows, fields, NT)
            for c in range(3):
                zbuf[:, p * 3 + c, :] = y[:, c * 128 : c * 128 + 128]
        per_order(ta)
        for c in range(3):
            for p in range(2):
                dst[:, c * 2 + p, :] = wbuf[:, p * 3 + c, :].T

    loads[0].wait()
    loads[1].wait()
    saved2 = split(saved[...])
    up2 = split(up[...])
    act[...] = dot3(saved2, up2, NN)
    loads[2].wait()
    loads[3].wait()
    gout2 = split(gout[...])
    gpre[...] = dot3(gout2, split(down[...]), NT)
    pre = act[...]
    scale = math.sqrt(2.0 / math.pi)
    square = pre * pre
    t = jnp.tanh(scale * (pre + 0.044715 * (square * pre)))
    half = 0.5 * (1.0 + t)
    act[...] = pre * half
    gpre[...] = gpre[...] * (
        half + (0.5 * scale) * pre * (1.0 - t * t) * (1.0 + (3.0 * 0.044715) * square)
    )
    field[...] = gout[...] + dot3(split(gpre[...]), up2, NT)
    to_channels(field, send1.at[1])
    pl.semaphore_wait(barrier, NDEV - 1)
    scatter(send1.at[1], recv1.at[1], 1)

    loads[4].wait()
    to_channels(x, send1.at[0])
    scatter(send1.at[0], recv1.at[0], 0)
    zbuf[...] = jnp.zeros_like(zbuf)

    def cut(first):
        for to in range(2):
            for k in range(6):

                def put(n, at, chip, count, step, to=to, k=k):
                    rows = pl.ds(6 * to + k + 12 * chip, count, stride=12 * step)
                    pieces[to, n, at : at + count, first + k, :] = part[n, rows, :]

                for i in range(4):
                    for low in range(2):
                        put(0, i * 16 + low * 8, low * 32 + i * 8, 8, 1)
                    for j in range(4):
                        put(1, i * 16 + j * 4, i % 2 * 32 + j * 8 + i // 2 * 4, 4, 1)
                    put(2, i * 16, i, 16, 4)

    def share_of(rows, columns, first):
        product = dot3(split(rows[...]), split(columns[...]), TN)
        for n in range(3):
            part[n] = product[:, n * 128 : n * 128 + 128]
        cut(first)

    share_of(gpre, saved, 0)
    share_of(act, gout, 6)
    partner = pltpu.make_async_remote_copy(
        src_ref=pieces.at[1 - core],
        dst_ref=pair,
        send_sem=psem.at[0],
        recv_sem=psem.at[1],
        device_id=(lat, lon + 1 - 2 * core),
        device_id_type=MESH,
    )
    partner.start()

    loads[5].wait()
    loads[6].wait()
    arrived(recv1.at[1], 1)
    analysis(recv1.at[1], send2.at[1])
    scatter(send2.at[1], recv2.at[1], 3)

    partner.wait()
    pair[...] = pair[...] + pieces[core]
    places = (x_at, y_at, z_at)

    def beside(n, step):
        if n == 0:
            return (y_lo * 4 + lax.rem(x_at + step, 4), lon)
        if n == 1:
            y = lax.rem(y_at + step, 4)
            return (lax.rem(y, 2) * 4 + x_at, (y // 2) * 8 + z_at * 2 + core)
        return (lat, y_hi * 8 + lax.rem(z_at + step, 4) * 2 + core)

    for step in (2, 1, 3):
        for n in range(3):
            to = lax.rem(places[n] + step, 4)
            pltpu.make_async_remote_copy(
                src_ref=pair.at[n, pl.ds(to * 16, 16)],
                dst_ref=ring.at[n, step - 1],
                send_sem=psem.at[2],
                recv_sem=psem.at[3],
                device_id=beside(n, step),
                device_id_type=MESH,
            ).start()

    arrived(recv1.at[0], 0)
    analysis(recv1.at[0], send2.at[0])
    scatter(send2.at[0], recv2.at[0], 2)

    loads[7].wait()
    arrived(recv2.at[1], 3)
    for c in range(3):
        for p in range(2):
            spec[1, c * 128 : c * 128 + 128, p * 128 : p * 128 + 128] = recv2[1, :, c * 2 + p, :]
    gspec2 = split(spec[1])
    coef = dot3(split(filt[...]), gspec2, NN)
    for c in range(3):
        for p in range(2):
            send3[:, c * 2 + p, :] = coef[c * 128 : c * 128 + 128, p * 128 : p * 128 + 128]
    scatter(send3, recv3, 4)

    pltpu.make_async_copy(ring, ring, psem.at[3]).wait()
    for n in range(3):
        own = pair[n, pl.ds(places[n] * 16, 16)]
        mid[n] = (own + ring[n, 0]) + (ring[n, 1] + ring[n, 2])
    planes = (y_lo * 8 + y_hi * 4 + z_at, x_at * 4 + z_at, y_lo * 8 + x_at * 2 + y_hi)

    def across(n, p):
        if n == 0:
            return ((p // 8) * 4 + x_at, lax.rem(p // 4, 2) * 8 + lax.rem(p, 4) * 2 + core)
        if n == 1:
            return (y_lo * 4 + p // 4, y_hi * 8 + lax.rem(p, 4) * 2 + core)
        return ((p // 8) * 4 + lax.rem(p // 2, 4), lax.rem(p, 2) * 8 + z_at * 2 + core)

    def spread(s, carry):
        for n in range(3):
            p = lax.rem(planes[n] + s, 16)
            pltpu.make_async_remote_copy(
                src_ref=mid.at[n, p],
                dst_ref=others.at[n, planes[n]],
                send_sem=osem.at[0],
                recv_sem=osem.at[1],
                device_id=across(n, p),
                device_id_type=MESH,
            ).start()
        return carry

    lax.fori_loop(1, 16, spread, 0)
    for n in range(3):
        pltpu.make_async_copy(mid.at[n, planes[n]], others.at[n, planes[n]], osem.at[1]).start()

    arrived(recv2.at[0], 2)
    for c in range(3):
        for p in range(2):
            spec[0, c * 128 : c * 128 + 128, p * 128 : p * 128 + 128] = recv2[0, :, c * 2 + p, :]
    gfil[...] = dot3(split(spec[0]), split(spec[1]), NT) * (
        1.0 / math.sqrt(2.0 * SAMPLES * MODES)
    )
    share = WIDTH // LAT

    def rows_of(d):
        return gfil.at[pl.ds(pl.multiple_of(d * share, 8), share)]

    def column(s, carry):
        d = lax.rem(lat + s, LAT)
        pltpu.make_async_remote_copy(
            src_ref=rows_of(d),
            dst_ref=gfrecv.at[lat],
            send_sem=gsem.at[0],
            recv_sem=gsem.at[1],
            device_id=(d, lon),
            device_id_type=MESH,
        ).start()
        return carry

    lax.fori_loop(1, LAT, column, 0)
    pltpu.make_async_copy(rows_of(lat), gfrecv.at[lat], gsem.at[1]).start()
    loads[8].wait()
    arrived(recv3, 4)
    for c in range(3):
        for p in range(2):
            zbuf[:, p * 3 + c, :] = recv3[:, c * 2 + p, :].T
    per_order(ts)
    for c in range(3):
        for p in range(2):
            spec[0, c * 128 : c * 128 + 128, p * 128 : p * 128 + 128] = wbuf[:, p * 3 + c, :].T
    grid = dot3(split(spec[0]), (fo[0], fo[1]), NN)
    circle[0] = grid[:, :128]
    circle[1] = grid[:, 128:]
    regroup_out(send4)
    scatter(send4, recv4, 5)

    pltpu.make_async_copy(others, others, osem.at[1]).wait()
    point_scale = 1.0 / math.sqrt(SAMPLES * NLAT * NLON)
    for n in range(3):
        total = jnp.sum(others[n], axis=0) * point_scale
        sums[0, :, n * 128 : n * 128 + 128] = total[:6]
        sums[1, :, n * 128 : n * 128 + 128] = total[6:]
    pltpu.make_async_copy(gfrecv, gfrecv, gsem.at[1]).wait()
    stores = [
        pltpu.make_async_copy(sums, up_out, out_sem.at[0]),
        pltpu.make_async_copy(gfrecv, gf_out, out_sem.at[1]),
    ]
    for store in stores:
        store.start()

    arrived(recv4, 5)
    for c in range(3):
        for h in range(2):
            rows, lanes = slice(h * 128, h * 128 + 128), slice(c * 128, c * 128 + 128)
            field[rows, lanes] = field[rows, lanes] + recv4[:, c * 2 + h, :].T
    last = pltpu.make_async_copy(field, gin_out, out_sem.at[2])
    last.start()

    sent(send1.at[0], 0)
    sent(send1.at[1], 1)
    sent(send2.at[0], 2)
    sent(send2.at[1], 3)
    sent(send3, 4)
    sent(send4, 5)
    pltpu.make_async_copy(ring, ring, psem.at[2]).wait()
    some = others.at[:, pl.ds(0, 15)]
    pltpu.make_async_copy(some, some, osem.at[0]).wait()
    some = gfil.at[pl.ds(0, WIDTH - share)]
    pltpu.make_async_copy(some, some, gsem.at[0]).wait()
    for store in stores:
        store.wait()
    last.wait()


def results(gin, sums, gfil, gin_out, up_out, down_out, gfil_out, a, b, c, sem, out_sem):
    loads = [
        pltpu.make_async_copy(gfil, c, sem.at[0]),
        pltpu.make_async_copy(gin, a, sem.at[1]),
        pltpu.make_async_copy(sums, b, sem.at[2]),
    ]
    pairs = [(c, gfil_out), (a, gin_out), (b.at[0], up_out), (b.at[1], down_out)]
    stores = [pltpu.make_async_copy(s, d, out_sem.at[i]) for i, (s, d) in enumerate(pairs)]
    for load in loads:
        load.start()
    for i, store in enumerate(stores):
        if i < 3:
            loads[i].wait()
        store.start()
    for store in stores:
        store.wait()


def shards(inputs, saved, grad_out, w_up, w_down, w_filter):
    legendre = legendre_values()
    device = np.arange(NDEV)
    legendre = legendre[:, (device % LON) * LAT + device // LON]
    ta = np.concatenate(halves(legendre.transpose(0, 2, 1)), axis=2)
    ts = np.concatenate(halves(legendre), axis=2)
    fo = np.stack(halves(fourier_values().T))
    anywhere = pl.BlockSpec(memory_space=pl.ANY)

    def block():
        return pltpu.VMEM((NDEV, 6, 128), F32)

    def blocks(n):
        return pltpu.VMEM((n, NDEV, 6, 128), F32)

    gin, sums, gfil = pl.pallas_call(
        kernel,
        out_shape=(
            jax.ShapeDtypeStruct((POINTS, WIDTH), F32),
            jax.ShapeDtypeStruct((2, 6, WIDTH), F32),
            jax.ShapeDtypeStruct((LAT, WIDTH // LAT, WIDTH), F32),
        ),
        in_specs=[anywhere] * 9,
        out_specs=(anywhere,) * 3,
        scratch_shapes=[
            pltpu.VMEM((POINTS, WIDTH), F32),
            pltpu.VMEM((POINTS, WIDTH), F32),
            pltpu.VMEM((POINTS, WIDTH), F32),
            pltpu.VMEM((WIDTH, HIDDEN), F32),
            pltpu.VMEM((HIDDEN, WIDTH), F32),
            pltpu.VMEM((WIDTH, WIDTH), F32),
            pltpu.VMEM((MODES, NLAT, 256), BF16),
            pltpu.VMEM((MODES, MODES, 256), BF16),
            pltpu.VMEM((2, 256, 256), BF16),
            blocks(2), blocks(2), blocks(2), blocks(2), block(), block(), block(), block(),
            pltpu.VMEM((POINTS, HIDDEN), F32),
            pltpu.VMEM((POINTS, HIDDEN), F32),
            pltpu.VMEM((POINTS, WIDTH), F32),
            pltpu.VMEM((3, HIDDEN, 128), F32),
            pltpu.VMEM((2, 3, NDEV // 2, 12, 128), F32),
            pltpu.VMEM((3, NDEV // 2, 12, 128), F32),
            pltpu.VMEM((3, 3, 16, 12, 128), F32),
            pltpu.VMEM((3, 16, 12, 128), F32),
            pltpu.VMEM((3, 16, 12, 128), F32),
            pltpu.VMEM((2, WIDTH, 128), F32),
            pltpu.VMEM((MODES, 8, 128), F32),
            pltpu.VMEM((MODES, 8, 128), F32),
            pltpu.VMEM((2, WIDTH, 256), F32),
            pltpu.VMEM((WIDTH, WIDTH), F32),
            pltpu.VMEM((LAT, WIDTH // LAT, WIDTH), F32),
            pltpu.VMEM((2, 6, WIDTH), F32),
            pltpu.SemaphoreType.DMA((9,)),
            pltpu.SemaphoreType.DMA((6,)),
            pltpu.SemaphoreType.DMA((6,)),
            pltpu.SemaphoreType.DMA((4,)),
            pltpu.SemaphoreType.DMA((2,)),
            pltpu.SemaphoreType.DMA((2,)),
            pltpu.SemaphoreType.DMA((3,)),
        ],
        compiler_params=pltpu.CompilerParams(
            collective_id=0, has_side_effects=True, vmem_limit_bytes=56 << 20
        ),
    )(
        inputs.reshape(POINTS, WIDTH), saved.reshape(POINTS, WIDTH),
        grad_out.reshape(POINTS, WIDTH), w_up, w_down, w_filter,
        jnp.asarray(ta), jnp.asarray(ts), jnp.asarray(fo),
    )
    gin, up, down, gfil = pl.pallas_call(
        results,
        out_shape=(
            jax.ShapeDtypeStruct((POINTS, WIDTH), F32),
            jax.ShapeDtypeStruct((6, WIDTH), F32),
            jax.ShapeDtypeStruct((6, WIDTH), F32),
            jax.ShapeDtypeStruct((LAT, WIDTH // LAT, WIDTH), F32),
        ),
        in_specs=[anywhere] * 3,
        out_specs=(anywhere,) * 4,
        scratch_shapes=[
            pltpu.VMEM((POINTS, WIDTH), F32),
            pltpu.VMEM((2, 6, WIDTH), F32),
            pltpu.VMEM((LAT, WIDTH // LAT, WIDTH), F32),
            pltpu.SemaphoreType.DMA((3,)),
            pltpu.SemaphoreType.DMA((4,)),
        ],
    )(gin, sums, gfil)
    return (gin.reshape(inputs.shape), up.T, down, gfil)


def solution(mesh):
    in_specs = (
        P(None, "lat", "lon", None),
        P(None, "lat", "lon", None),
        P(None, "lat", "lon", None),
        P(),
        P(),
        P("lon", None, None),
    )
    out_specs = (
        P(None, "lat", "lon", None),
        P(None, ("lat", "lon")),
        P(("lat", "lon"), None),
        P("lon", "lat", None),
    )
    return jax.shard_map(shards, mesh=mesh, in_specs=in_specs, out_specs=out_specs, check_vma=False)
```

```python
import math

import jax
import jax.numpy as jnp
import numpy as np
from jax import lax
from jax.experimental import pallas as pl
from jax.experimental.pallas import tpu as pltpu
from jax.sharding import PartitionSpec as P

NLAT = 128
NLON = 256
MODES = 128
WIDTH = 384
HIDDEN = 768
SAMPLES = 1
NDEV = 128
LON = 16
LAT = 8
POINTS = 256
BLOCK = 64
AWAY = (0, 1, 2, 1)
STEPS = sorted(
    [(i // 32, i // 8 % 4, i // 2 % 4, i % 2) for i in range(1, NDEV)],
    key=lambda step: -sum(AWAY[k] for k in step[:3]),
)
MESH = pl.DeviceIdType.MESH
F32 = jnp.float32
BF16 = jnp.bfloat16

NN = (((1,), (0,)), ((), ()))
NT = (((1,), (1,)), ((), ()))
TN = (((0,), (0,)), ((), ()))


def legendre_values():
    theta = np.pi * (np.arange(NLAT) + 0.5) / NLAT
    cosines, sines = np.cos(theta), np.sin(theta)
    order = np.arange(MODES, dtype=np.float64)[:, None]
    k = np.arange(1, MODES, dtype=np.float64)
    log_prod = np.concatenate([[0.0], np.cumsum(np.log((2 * k - 1) / (2 * k)))])
    initial = np.exp(
        0.5 * np.log((2 * order + 1) / (4 * np.pi))
        + 0.5 * log_prod[:, None]
        + order * np.log(sines)[None, :]
    )
    previous = np.zeros((MODES, NLAT))
    earlier = np.zeros((MODES, NLAT))
    rows = []
    for degree in range(MODES):
        l = float(degree)
        a = np.sqrt(np.maximum(4 * l * l - 1, 1) / np.maximum(l * l - order * order, 1))
        b = np.sqrt(
            np.maximum((l - 1) ** 2 - order * order, 0) / np.maximum(4 * (l - 1) ** 2 - 1, 1)
        )
        grown = a * (cosines[None, :] * previous - b * earlier)
        current = np.where(order == l, initial, np.where(order < l, grown, 0.0))
        previous, earlier = current, previous
        rows.append(current)
    table = np.stack(rows, axis=1)
    return table * np.sqrt(2 * np.pi * np.pi * sines / NLAT)[None, None, :]


def fourier_values():
    phase = (np.arange(NLON)[:, None] * np.arange(MODES)[None, :]) % NLON
    angle = 2 * np.pi * phase / NLON
    return np.concatenate([np.cos(angle), -np.sin(angle)], axis=1) * np.sqrt(2.0 / NLON)


def halves(table):
    table = np.asarray(table, np.float32)
    high = table.astype(jnp.bfloat16)
    low = (table - high.astype(np.float32)).astype(jnp.bfloat16)
    return high, low


def split(x):
    high = x.astype(BF16)
    return high, (x - high.astype(F32)).astype(BF16)


def dot3(a, b, dims):
    def dot(u, v):
        return lax.dot_general(u, v, dims, preferred_element_type=F32)

    return dot(a[0], b[0]) + (dot(a[0], b[1]) + dot(a[1], b[0]))


def exchange(tiles, lane):
    tiles = list(tiles)
    for bit in (1, 2, 4):
        upper = jnp.bitwise_and(lane, 16 * bit) != 0
        for s in range(8):
            if s & bit:
                continue
            lo, hi = tiles[s], tiles[s | bit]
            tiles[s] = jnp.where(upper, pltpu.roll(hi, 16 * bit, 1), lo)
            tiles[s | bit] = jnp.where(upper, hi, pltpu.roll(lo, 128 - 16 * bit, 1))
    return tiles


def kernel(
    x_hbm, saved_hbm, gout_hbm, up_hbm, down_hbm, filt_hbm, ta_hbm, ts_hbm, fo_hbm,
    gin_out, up_out, gf_out,
    x, saved, gout, up, down, filt, ta, ts, fo,
    send1, recv1, send2, recv2, send3, recv3, send4, recv4,
    act, gpre, field, part, pieces, pair, ring, mid, others, circle, zbuf, wbuf, spec, gfil, gfrecv, sums,
    load_sem, ssem, rsem, psem, osem, gsem, out_sem,
):
    lat = lax.axis_index("lat")
    lon = lax.axis_index("lon")
    me = lat * LON + lon
    core = lax.rem(lon, 2)

    def by_place(d):
        return (d // LON, lax.rem(d, LON))

    x_at, y_lo = lax.rem(lat, 4), lat // 4
    z_at, y_hi = lax.rem(lon // 2, 4), lon // 8
    y_at = y_hi * 2 + y_lo
    ys = [lax.rem(y_at + i, 4) for i in range(4)]
    lats = [[lax.rem(y, 2) * 4 + lax.rem(x_at + i, 4) for i in range(4)] for y in ys]
    lons = [
        [
            [(y // 2) * 8 + lax.rem(z_at + i, 4) * 2 + lax.rem(core + c, 2) for c in range(2)]
            for i in range(4)
        ]
        for y in ys
    ]

    barrier = pltpu.get_barrier_semaphore()

    def greet(s, carry):
        pl.semaphore_signal(
            barrier, inc=1, device_id=by_place(lax.rem(me + s, NDEV)), device_id_type=MESH
        )
        return carry

    lax.fori_loop(1, NDEV, greet, 0)

    pairs = [
        (saved_hbm, saved), (up_hbm, up), (gout_hbm, gout), (down_hbm, down), (x_hbm, x),
        (fo_hbm, fo), (ta_hbm, ta), (filt_hbm.at[lat], filt), (ts_hbm, ts),
    ]
    loads = [pltpu.make_async_copy(s, d, load_sem.at[i]) for i, (s, d) in enumerate(pairs)]
    for load in loads:
        load.start()

    def scatter(src, dst, n):
        for y, x_, z, c in STEPS:
            to_lat = lats[y][x_]
            to_lon = lons[y][z][c]
            pltpu.make_async_remote_copy(
                src_ref=src.at[to_lat * LON + to_lon],
                dst_ref=dst.at[me],
                send_sem=ssem.at[n],
                recv_sem=rsem.at[n],
                device_id=(to_lat, to_lon),
                device_id_type=MESH,
            ).start()
        pltpu.make_async_copy(src.at[me], dst.at[me], rsem.at[n]).start()

    def arrived(dst, n):
        pltpu.make_async_copy(dst, dst, rsem.at[n]).wait()

    def sent(src, n):
        some = src.at[pl.ds(0, NDEV - 1)]
        pltpu.make_async_copy(some, some, ssem.at[n]).wait()

    lane = lax.broadcasted_iota(jnp.int32, (8, 128), 1)

    def to_channels(values, dst):
        for c in range(3):
            for h in range(2):
                block = values[h * 128 : h * 128 + 128, c * 128 : c * 128 + 128]
                dst[:, c * 2 + h, :] = block.T

    def regroup_in(src):
        for c in range(3):
            for h in range(2):
                for top in range(2):
                    tiles = [
                        src[pl.ds(top * 8 + s, 8, stride=16), c * 2 + h, :] for s in range(8)
                    ]
                    for s, tile in enumerate(exchange(tiles, lane)):
                        circle[top, pl.ds(c * 128 + h * 8 + s, 8, stride=16), :] = tile

    def regroup_out(dst):
        for c in range(3):
            for h in range(2):
                for top in range(2):
                    tiles = [
                        circle[top, pl.ds(c * 128 + h * 8 + s, 8, stride=16), :]
                        for s in range(8)
                    ]
                    for s, tile in enumerate(exchange(tiles, lane)):
                        dst[pl.ds(top * 8 + s, 8, stride=16), c * 2 + h, :] = tile

    def per_order(table):
        def several(i, carry):
            for u in range(BLOCK):
                m = i * BLOCK + u
                z = zbuf[m]
                high = z.astype(BF16).astype(F32)
                rows = jnp.concatenate([high, z - high], axis=0).astype(BF16)
                r = lax.dot_general(rows, table[m], NN, preferred_element_type=F32)
                wbuf[m] = r[:8, :128] + (r[:8, 128:] + r[8:, :128])
            return carry

        lax.fori_loop(0, MODES // BLOCK, several, 0)

    def analysis(src, dst):
        regroup_in(src)
        fields = split(jnp.concatenate([circle[0], circle[1]], axis=1))
        for p in range(2):
            rows = (fo[0, p * 128 : p * 128 + 128], fo[1, p * 128 : p * 128 + 128])
            y = dot3(rows, fields, NT)
            for c in range(3):
                zbuf[:, p * 3 + c, :] = y[:, c * 128 : c * 128 + 128]
        per_order(ta)
        for c in range(3):
            for p in range(2):
                dst[:, c * 2 + p, :] = wbuf[:, p * 3 + c, :].T

    loads[0].wait()
    loads[1].wait()
    saved2 = split(saved[...])
    up2 = split(up[...])
    act[...] = dot3(saved2, up2, NN)
    loads[2].wait()
    loads[3].wait()
    gout2 = split(gout[...])
    gpre[...] = dot3(gout2, split(down[...]), NT)
    pre = act[...]
    scale = math.sqrt(2.0 / math.pi)
    square = pre * pre
    t = jnp.tanh(scale * (pre + 0.044715 * (square * pre)))
    half = 0.5 * (1.0 + t)
    act[...] = pre * half
    gpre[...] = gpre[...] * (
        half + (0.5 * scale) * pre * (1.0 - t * t) * (1.0 + (3.0 * 0.044715) * square)
    )
    field[...] = gout[...] + dot3(split(gpre[...]), up2, NT)
    to_channels(field, send1.at[1])
    pl.semaphore_wait(barrier, NDEV - 1)
    scatter(send1.at[1], recv1.at[1], 1)

    loads[4].wait()
    to_channels(x, send1.at[0])
    scatter(send1.at[0], recv1.at[0], 0)
    zbuf[...] = jnp.zeros_like(zbuf)

    def cut(first):
        for to in range(2):
            for k in range(6):

                def put(n, at, chip, count, step, to=to, k=k):
                    rows = pl.ds(6 * to + k + 12 * chip, count, stride=12 * step)
                    pieces[to, n, at : at + count, first + k, :] = part[n, rows, :]

                for i in range(4):
                    for low in range(2):
                        put(0, i * 16 + low * 8, low * 32 + i * 8, 8, 1)
                    for j in range(4):
                        put(1, i * 16 + j * 4, i % 2 * 32 + j * 8 + i // 2 * 4, 4, 1)
                    put(2, i * 16, i, 16, 4)

    def share_of(rows, columns, first):
        product = dot3(split(rows[...]), split(columns[...]), TN)
        for n in range(3):
            part[n] = product[:, n * 128 : n * 128 + 128]
        cut(first)

    share_of(gpre, saved, 0)
    share_of(act, gout, 6)
    partner = pltpu.make_async_remote_copy(
        src_ref=pieces.at[1 - core],
        dst_ref=pair,
        send_sem=psem.at[0],
        recv_sem=psem.at[1],
        device_id=(lat, lon + 1 - 2 * core),
        device_id_type=MESH,
    )
    partner.start()

    loads[5].wait()
    loads[6].wait()
    arrived(recv1.at[1], 1)
    analysis(recv1.at[1], send2.at[1])
    scatter(send2.at[1], recv2.at[1], 3)

    partner.wait()
    pair[...] = pair[...] + pieces[core]
    places = (x_at, y_at, z_at)

    def beside(n, step):
        if n == 0:
            return (y_lo * 4 + lax.rem(x_at + step, 4), lon)
        if n == 1:
            y = lax.rem(y_at + step, 4)
            return (lax.rem(y, 2) * 4 + x_at, (y // 2) * 8 + z_at * 2 + core)
        return (lat, y_hi * 8 + lax.rem(z_at + step, 4) * 2 + core)

    for step in (2, 1, 3):
        for n in range(3):
            to = lax.rem(places[n] + step, 4)
            pltpu.make_async_remote_copy(
                src_ref=pair.at[n, pl.ds(to * 16, 16)],
                dst_ref=ring.at[n, step - 1],
                send_sem=psem.at[2],
                recv_sem=psem.at[3],
                device_id=beside(n, step),
                device_id_type=MESH,
            ).start()

    arrived(recv1.at[0], 0)
    analysis(recv1.at[0], send2.at[0])
    scatter(send2.at[0], recv2.at[0], 2)

    loads[7].wait()
    filt2 = split(filt[...])
    arrived(recv2.at[1], 3)
    for c in range(3):
        for p in range(2):
            spec[1, c * 128 : c * 128 + 128, p * 128 : p * 128 + 128] = recv2[1, :, c * 2 + p, :]
    gspec2 = split(spec[1])
    coef = dot3(filt2, gspec2, NN)
    for c in range(3):
        for p in range(2):
            send3[:, c * 2 + p, :] = coef[c * 128 : c * 128 + 128, p * 128 : p * 128 + 128]
    scatter(send3, recv3, 4)

    pltpu.make_async_copy(ring, ring, psem.at[3]).wait()
    for n in range(3):
        own = pair[n, pl.ds(places[n] * 16, 16)]
        mid[n] = (own + ring[n, 0]) + (ring[n, 1] + ring[n, 2])
    planes = (y_lo * 8 + y_hi * 4 + z_at, x_at * 4 + z_at, y_lo * 8 + x_at * 2 + y_hi)

    def across(n, p):
        if n == 0:
            return ((p // 8) * 4 + x_at, lax.rem(p // 4, 2) * 8 + lax.rem(p, 4) * 2 + core)
        if n == 1:
            return (y_lo * 4 + p // 4, y_hi * 8 + lax.rem(p, 4) * 2 + core)
        return ((p // 8) * 4 + lax.rem(p // 2, 4), lax.rem(p, 2) * 8 + z_at * 2 + core)

    def spread(s, carry):
        for n in range(3):
            p = lax.rem(planes[n] + s, 16)
            pltpu.make_async_remote_copy(
                src_ref=mid.at[n, p],
                dst_ref=others.at[n, planes[n]],
                send_sem=osem.at[0],
                recv_sem=osem.at[1],
                device_id=across(n, p),
                device_id_type=MESH,
            ).start()
        return carry

    lax.fori_loop(1, 16, spread, 0)
    for n in range(3):
        pltpu.make_async_copy(mid.at[n, planes[n]], others.at[n, planes[n]], osem.at[1]).start()

    arrived(recv2.at[0], 2)
    for c in range(3):
        for p in range(2):
            spec[0, c * 128 : c * 128 + 128, p * 128 : p * 128 + 128] = recv2[0, :, c * 2 + p, :]
    gfil[...] = dot3(split(spec[0]), split(spec[1]), NT) * (
        1.0 / math.sqrt(2.0 * SAMPLES * MODES)
    )
    share = WIDTH // LAT

    def rows_of(d):
        return gfil.at[pl.ds(pl.multiple_of(d * share, 8), share)]

    def column(s, carry):
        d = lax.rem(lat + s, LAT)
        pltpu.make_async_remote_copy(
            src_ref=rows_of(d),
            dst_ref=gfrecv.at[lat],
            send_sem=gsem.at[0],
            recv_sem=gsem.at[1],
            device_id=(d, lon),
            device_id_type=MESH,
        ).start()
        return carry

    lax.fori_loop(1, LAT, column, 0)
    pltpu.make_async_copy(rows_of(lat), gfrecv.at[lat], gsem.at[1]).start()
    loads[8].wait()
    arrived(recv3, 4)
    for c in range(3):
        for p in range(2):
            zbuf[:, p * 3 + c, :] = recv3[:, c * 2 + p, :].T
    per_order(ts)
    for c in range(3):
        for p in range(2):
            spec[0, c * 128 : c * 128 + 128, p * 128 : p * 128 + 128] = wbuf[:, p * 3 + c, :].T
    grid = dot3(split(spec[0]), (fo[0], fo[1]), NN)
    circle[0] = grid[:, :128]
    circle[1] = grid[:, 128:]
    regroup_out(send4)
    scatter(send4, recv4, 5)

    pltpu.make_async_copy(others, others, osem.at[1]).wait()
    point_scale = 1.0 / math.sqrt(SAMPLES * NLAT * NLON)
    for n in range(3):
        total = jnp.sum(others[n], axis=0) * point_scale
        sums[0, :, n * 128 : n * 128 + 128] = total[:6]
        sums[1, :, n * 128 : n * 128 + 128] = total[6:]
    pltpu.make_async_copy(gfrecv, gfrecv, gsem.at[1]).wait()
    stores = [
        pltpu.make_async_copy(sums, up_out, out_sem.at[0]),
        pltpu.make_async_copy(gfrecv, gf_out, out_sem.at[1]),
    ]
    for store in stores:
        store.start()

    arrived(recv4, 5)
    for c in range(3):
        for h in range(2):
            rows, lanes = slice(h * 128, h * 128 + 128), slice(c * 128, c * 128 + 128)
            field[rows, lanes] = field[rows, lanes] + recv4[:, c * 2 + h, :].T
    last = pltpu.make_async_copy(field, gin_out, out_sem.at[2])
    last.start()

    sent(send1.at[0], 0)
    sent(send1.at[1], 1)
    sent(send2.at[0], 2)
    sent(send2.at[1], 3)
    sent(send3, 4)
    sent(send4, 5)
    pltpu.make_async_copy(ring, ring, psem.at[2]).wait()
    some = others.at[:, pl.ds(0, 15)]
    pltpu.make_async_copy(some, some, osem.at[0]).wait()
    some = gfil.at[pl.ds(0, WIDTH - share)]
    pltpu.make_async_copy(some, some, gsem.at[0]).wait()
    for store in stores:
        store.wait()
    last.wait()


def results(gin, sums, gfil, gin_out, up_out, down_out, gfil_out, a, b, c, sem, out_sem):
    loads = [
        pltpu.make_async_copy(gfil, c, sem.at[0]),
        pltpu.make_async_copy(gin, a, sem.at[1]),
        pltpu.make_async_copy(sums, b, sem.at[2]),
    ]
    pairs = [(c, gfil_out), (a, gin_out), (b.at[0], up_out), (b.at[1], down_out)]
    stores = [pltpu.make_async_copy(s, d, out_sem.at[i]) for i, (s, d) in enumerate(pairs)]
    for load in loads:
        load.start()
    for i, store in enumerate(stores):
        if i < 3:
            loads[i].wait()
        store.start()
    for store in stores:
        store.wait()


def shards(inputs, saved, grad_out, w_up, w_down, w_filter):
    legendre = legendre_values()
    device = np.arange(NDEV)
    legendre = legendre[:, (device % LON) * LAT + device // LON]
    ta = np.concatenate(halves(legendre.transpose(0, 2, 1)), axis=2)
    ts = np.concatenate(halves(legendre), axis=2)
    fo = np.stack(halves(fourier_values().T))
    anywhere = pl.BlockSpec(memory_space=pl.ANY)

    def block():
        return pltpu.VMEM((NDEV, 6, 128), F32)

    def blocks(n):
        return pltpu.VMEM((n, NDEV, 6, 128), F32)

    gin, sums, gfil = pl.pallas_call(
        kernel,
        out_shape=(
            jax.ShapeDtypeStruct((POINTS, WIDTH), F32),
            jax.ShapeDtypeStruct((2, 6, WIDTH), F32),
            jax.ShapeDtypeStruct((LAT, WIDTH // LAT, WIDTH), F32),
        ),
        in_specs=[anywhere] * 9,
        out_specs=(anywhere,) * 3,
        scratch_shapes=[
            pltpu.VMEM((POINTS, WIDTH), F32),
            pltpu.VMEM((POINTS, WIDTH), F32),
            pltpu.VMEM((POINTS, WIDTH), F32),
            pltpu.VMEM((WIDTH, HIDDEN), F32),
            pltpu.VMEM((HIDDEN, WIDTH), F32),
            pltpu.VMEM((WIDTH, WIDTH), F32),
            pltpu.VMEM((MODES, NLAT, 256), BF16),
            pltpu.VMEM((MODES, MODES, 256), BF16),
            pltpu.VMEM((2, 256, 256), BF16),
            blocks(2), blocks(2), blocks(2), blocks(2), block(), block(), block(), block(),
            pltpu.VMEM((POINTS, HIDDEN), F32),
            pltpu.VMEM((POINTS, HIDDEN), F32),
            pltpu.VMEM((POINTS, WIDTH), F32),
            pltpu.VMEM((3, HIDDEN, 128), F32),
            pltpu.VMEM((2, 3, NDEV // 2, 12, 128), F32),
            pltpu.VMEM((3, NDEV // 2, 12, 128), F32),
            pltpu.VMEM((3, 3, 16, 12, 128), F32),
            pltpu.VMEM((3, 16, 12, 128), F32),
            pltpu.VMEM((3, 16, 12, 128), F32),
            pltpu.VMEM((2, WIDTH, 128), F32),
            pltpu.VMEM((MODES, 8, 128), F32),
            pltpu.VMEM((MODES, 8, 128), F32),
            pltpu.VMEM((2, WIDTH, 256), F32),
            pltpu.VMEM((WIDTH, WIDTH), F32),
            pltpu.VMEM((LAT, WIDTH // LAT, WIDTH), F32),
            pltpu.VMEM((2, 6, WIDTH), F32),
            pltpu.SemaphoreType.DMA((9,)),
            pltpu.SemaphoreType.DMA((6,)),
            pltpu.SemaphoreType.DMA((6,)),
            pltpu.SemaphoreType.DMA((4,)),
            pltpu.SemaphoreType.DMA((2,)),
            pltpu.SemaphoreType.DMA((2,)),
            pltpu.SemaphoreType.DMA((3,)),
        ],
        compiler_params=pltpu.CompilerParams(
            collective_id=0, has_side_effects=True, vmem_limit_bytes=56 << 20
        ),
    )(
        inputs.reshape(POINTS, WIDTH), saved.reshape(POINTS, WIDTH),
        grad_out.reshape(POINTS, WIDTH), w_up, w_down, w_filter,
        jnp.asarray(ta), jnp.asarray(ts), jnp.asarray(fo),
    )
    gin, up, down, gfil = pl.pallas_call(
        results,
        out_shape=(
            jax.ShapeDtypeStruct((POINTS, WIDTH), F32),
            jax.ShapeDtypeStruct((6, WIDTH), F32),
            jax.ShapeDtypeStruct((6, WIDTH), F32),
            jax.ShapeDtypeStruct((LAT, WIDTH // LAT, WIDTH), F32),
        ),
        in_specs=[anywhere] * 3,
        out_specs=(anywhere,) * 4,
        scratch_shapes=[
            pltpu.VMEM((POINTS, WIDTH), F32),
            pltpu.VMEM((2, 6, WIDTH), F32),
            pltpu.VMEM((LAT, WIDTH // LAT, WIDTH), F32),
            pltpu.SemaphoreType.DMA((3,)),
            pltpu.SemaphoreType.DMA((4,)),
        ],
    )(gin, sums, gfil)
    return (gin.reshape(inputs.shape), up.T, down, gfil)


def solution(mesh):
    in_specs = (
        P(None, "lat", "lon", None),
        P(None, "lat", "lon", None),
        P(None, "lat", "lon", None),
        P(),
        P(),
        P("lon", None, None),
    )
    out_specs = (
        P(None, "lat", "lon", None),
        P(None, ("lat", "lon")),
        P(("lat", "lon"), None),
        P("lon", "lat", None),
    )
    return jax.shard_map(shards, mesh=mesh, in_specs=in_specs, out_specs=out_specs, check_vma=False)
```
